512 devices in a mesh: seq: 32 (over x, z), tensor: 16 (over y, core).
Axes of the slice: x: 4, y: 8, z: 8, core: 2. Of those that a mesh axis runs over, the one named last changes fastest.
Arguments:
- text_hidden: bfloat16 [4096, 8192], P('seq', 'tensor'), may hold values from -1500 to 1500
- patches: bfloat16 [4096, 8192], P('seq', 'tensor'), may hold values from -1500 to 1500
- norm_gain: float32 [8192], replicated, may hold values from 0.5 to 1.5
- head_weight: bfloat16 [152064, 8192], P(('seq', 'tensor')), may hold values from -2 to 2
- image_rows: int32 [4096], P('seq'), may hold values from -1 to 4095, as said below
- patch_owner: int32 [4096], P('seq'), may hold values from -1 to 4095, as said below
- nucleus: int32 [4096, 32], P('seq'), may hold values from 0 to 511, as said below
- sampled_code: int32 [4096], P('seq'), may hold values from 0 to 9503
Outputs:
- logprob: float32 [4096], P('seq')
The draws below stay inside these ranges and needn't reach their ends.
Inputs may be any that keep to these rules, and one draw needn't show every extreme that they name: `image_rows`: image tokens come in aligned blocks of 64 positions, filled in order by 64 consecutive patch rows that start at a multiple of 64 within one encoder shard's 128 rows; the images of one sequence shard come from different encoder shards; some sequence shard is all image tokens. The inverse of image_rows: patch row q fills token patch_owner[q], or none for -1. `nucleus`: A token's 32 blocks are distinct. Among the rows of one sequence shard (aligned blocks of 128 rows) no block appears more than 10 times, and some block appears exactly 10 times in every shard.
All inputs are finite; a program needn't handle non-finite values.
Results may differ from the reference program's by a relative error of at most 0.00078.
Values may be sent and summed in bfloat16 or wider, within the bound.
No kernel may reach another device: no remote copies, remote signals or barrier semaphores. Data moves between devices by JAX's collectives and lax.ppermute only.
A program may use at most 64 MiB of HBM per device.

```python
import math
import jax
import jax.numpy as jnp
from jax import lax

D = 8192
VB = 297
IMG = 64
TOK_DEV = 128
SHARDS = 32
NB = 32
BLOCKS = 512
CAP = 10
SLOTS = 2
TOKENS = 4096
PATCHES = 4096
VOCAB = 152064


def column_scales(key, rise):
    scale_key = jax.random.fold_in(key, 101)
    spread = jnp.exp(jax.random.uniform(scale_key, (D,), jnp.float32, 0.0, math.log(10.0)))
    ramp = jnp.arange(D, dtype=jnp.float32) / D
    return spread * jnp.power(jnp.float32(rise), ramp)


def feature_rows(key, salt, rise):
    columns = column_scales(key, rise)
    row_key = jax.random.fold_in(key, salt)
    lookup_entries, key_gauss = jax.random.split(row_key, 2)
    row_scale = jnp.exp(jax.random.uniform(lookup_entries, (TOKENS,), jnp.float32, 0.0, math.log(10.0)))
    gauss = jnp.clip(jax.random.normal(key_gauss, (TOKENS, D), jnp.float32), -4.0, 4.0)
    basis = gauss
    return row_scale[:, None] * columns[None, :] * basis


def layout(key):
    own = jax.random.fold_in(key, 11)
    key_count, key_perm, key_rank = jax.random.split(own, 3)
    shard_ids = jnp.arange(SHARDS, dtype=jnp.int32)
    slot_ids = jnp.arange(SLOTS, dtype=jnp.int32)
    spread_perm = jax.random.permutation(key_perm, SHARDS - 1).astype(jnp.int32)
    spread_perm = spread_perm + (spread_perm >= SHARDS // 2).astype(jnp.int32)
    distances = jnp.concatenate([jnp.full((1,), SHARDS // 2, jnp.int32), spread_perm[:SLOTS - 1]])
    heavy = (SHARDS - 1 - distances[SLOTS - 1]) % SHARDS
    counts = jax.random.randint(key_count, (SHARDS,), 0, SLOTS + 1)
    counts = jnp.where(shard_ids == SHARDS - 1, jnp.maximum(counts, 1), counts)
    counts = jnp.where(shard_ids == heavy, SLOTS, counts).astype(jnp.int32)
    rating_numbers = jax.random.randint(key_rank, (SHARDS, SLOTS), 0, 4096) * SLOTS + slot_ids[None, :]
    forced = (shard_ids[:, None] == SHARDS - 1) & (slot_ids[None, :] == SLOTS - 1)
    rating_numbers = jnp.where(forced, -1, rating_numbers)
    ranking = jnp.argsort(jnp.argsort(rating_numbers, axis=1), axis=1).astype(jnp.int32)
    is_image = ranking < counts[:, None]
    source = (shard_ids[:, None] + distances[ranking]) % SHARDS
    start = source * TOK_DEV + ranking * IMG
    embedding_lines = start[:, :, None] + jnp.arange(IMG)[None, None, :]
    image_rows = jnp.where(is_image[:, :, None], embedding_lines, -1).reshape(TOKENS).astype(jnp.int32)
    place = jnp.where(image_rows >= 0, image_rows, PATCHES).astype(jnp.int32)
    owners = jnp.full((PATCHES,), -1, jnp.int32).at[place].set(jnp.arange(TOKENS, dtype=jnp.int32), mode='drop')
    return (image_rows, owners)


def routing(key):
    own = jax.random.fold_in(key, 23)
    key_popular, key_hot, key_shards = jax.random.split(own, 3)
    popular = (jax.random.randint(key_popular, (BLOCKS,), 0, 8) == 0).astype(jnp.int32)
    hottest = jax.random.randint(key_hot, (), 0, BLOCKS)
    numbers = jnp.arange(BLOCKS, dtype=jnp.int32)

    def one_shard(shard_key):
        key_score, key_cut, key_perm = jax.random.split(shard_key, 3)
        base = jax.random.randint(key_score, (BLOCKS,), 0, 4096) + 4096 * popular + 8192 * (numbers == hottest).astype(jnp.int32)
        keyed = base * BLOCKS + numbers
        order = jnp.argsort(-keyed).astype(jnp.int32)
        cut = jax.random.randint(key_cut, (BLOCKS,), 0, CAP // 4 + 1)
        counts = jnp.where(numbers % 2 == 0, CAP, CAP - cut)
        cumulative = jnp.cumsum(counts)
        element = jnp.arange(TOK_DEV * NB, dtype=jnp.int32)
        index = jnp.searchsorted(cumulative, element, side='right')
        grid = order[index].reshape(NB, TOK_DEV).T
        shuffle = jax.random.permutation(key_perm, TOK_DEV)
        return grid[shuffle]
    return jax.vmap(one_shard)(jax.random.split(key_shards, SHARDS)).reshape(TOKENS, NB).astype(jnp.int32)


def draw_text_hidden(key, part):
    values = feature_rows(key, 202, math.sqrt(3.0))
    return values.astype(jnp.bfloat16)


def draw_patches(key, part):
    values = feature_rows(key, 303, math.sqrt(3.0))
    return values.astype(jnp.bfloat16)


def draw_head_weight(key, part):
    own = jax.random.fold_in(key, 5)
    key_bulk = jax.random.fold_in(own, 0)
    return (jnp.clip(jax.random.normal(key_bulk, (VOCAB, D), jnp.float32), -4.0, 4.0) * (3.5 / math.sqrt(D))).astype(jnp.bfloat16)


def draw_image_rows(key, part):
    image_rows, owners = layout(key)
    return image_rows


def draw_patch_owner(key, part):
    image_rows, owners = layout(key)
    return owners


def draw_nucleus(key, part):
    return routing(key)


def plant(drawn, own_key, smallest, top_value):
    spot = [jax.random.randint(jax.random.fold_in(own_key, axis), (), 0, length) for axis, length in enumerate(drawn.shape)]
    widest = drawn.shape.index(max(drawn.shape))
    beside = spot[:widest] + [(spot[widest] + 1) % drawn.shape[widest]] + spot[widest + 1:]
    return drawn.at[tuple(spot)].set(smallest).at[tuple(beside)].set(top_value)


def setup_inputs(seed: int = 0) -> dict:
    arg_keys = jax.random.split(jax.random.key(seed), 9)
    return {
        "text_hidden": draw_text_hidden(jax.random.fold_in(arg_keys[8], 71), 0),
        "patches": draw_patches(jax.random.fold_in(arg_keys[8], 71), 0),
        "norm_gain": jnp.clip(1.0 + 0.1 * jax.random.normal(arg_keys[2], (D,), jnp.float32), 0.5, 1.5),
        "head_weight": draw_head_weight(jax.random.fold_in(arg_keys[8], 71), 0),
        "image_rows": draw_image_rows(jax.random.fold_in(arg_keys[8], 71), 0),
        "patch_owner": draw_patch_owner(jax.random.fold_in(arg_keys[8], 71), 0),
        "nucleus": draw_nucleus(jax.random.fold_in(arg_keys[8], 71), 0),
        "sampled_code": plant(jax.random.randint(arg_keys[7], (TOKENS,), 0, NB * VB), jax.random.fold_in(arg_keys[7], 1), 0, (NB * VB) - 1).astype(jnp.int32),
    }


sharpness_divisor = 0.7
epsilon = 1e-06

def reference(text_hidden, patches, norm_gain, head_weight, image_rows, patch_owner, nucleus, sampled_code):
    place = jnp.where(patch_owner >= 0, patch_owner, TOKENS).astype(jnp.int32)
    scattered = jnp.zeros_like(text_hidden).at[place].set(patches, mode='drop')
    merged = jnp.where(image_rows[:, None] >= 0, scattered, text_hidden)
    values = merged.astype(jnp.float32)
    mean_square = lax.optimization_barrier(jnp.mean(values * values, axis=-1, keepdims=True))
    normed = (values * lax.rsqrt(mean_square + epsilon) * norm_gain.astype(jnp.float32)).astype(jnp.bfloat16)
    flat = nucleus.reshape(-1).astype(jnp.int32)
    pairs = flat.shape[0]
    order = jnp.argsort(flat, stable=True).astype(jnp.int32)
    ordered = flat[order]
    first = jnp.searchsorted(ordered, jnp.arange(BLOCKS, dtype=jnp.int32), side='left').astype(jnp.int32)
    position = (jnp.arange(pairs, dtype=jnp.int32) - first[ordered]).astype(jnp.int32)
    wide = SHARDS * CAP
    table = jnp.full((BLOCKS, wide), pairs, jnp.int32).at[ordered, position].set(order)
    token_of = (jnp.arange(pairs, dtype=jnp.int32) // NB).astype(jnp.int32)
    entry_of = (jnp.arange(pairs, dtype=jnp.int32) % NB).astype(jnp.int32)
    code = sampled_code[token_of]
    offset_of = jnp.where(entry_of == code // VB, code % VB, -1).astype(jnp.int32)

    def one_block(inputs):
        block, group_members = inputs
        safe = jnp.minimum(group_members, pairs - 1).astype(jnp.int32)
        embedding_lines = normed[token_of[safe]].astype(jnp.float32)
        coefficient_matrix = lax.dynamic_slice_in_dim(head_weight, (block * VB).astype(jnp.int32), VB, 0).astype(jnp.float32)
        rating_numbers = jnp.dot(embedding_lines, coefficient_matrix.T, precision=lax.Precision.HIGHEST, preferred_element_type=jnp.float32) / sharpness_divisor
        peak = lax.optimization_barrier(jnp.max(rating_numbers, axis=-1))
        total = lax.optimization_barrier(jnp.sum(jnp.exp(rating_numbers - peak[:, None]), axis=-1))
        column = lax.broadcasted_iota(jnp.int32, rating_numbers.shape, 1)
        picked = lax.optimization_barrier(jnp.sum(jnp.where(column == offset_of[safe][:, None], rating_numbers, 0.0), axis=-1))
        return (peak, total, picked)
    peaks, totals, picks = lax.map(one_block, (jnp.arange(BLOCKS, dtype=jnp.int32), table))
    target = table.reshape(-1)
    pair_peak = jnp.zeros((pairs,), jnp.float32).at[target].set(peaks.reshape(-1), mode='drop').reshape(TOKENS, NB)
    pair_total = jnp.zeros((pairs,), jnp.float32).at[target].set(totals.reshape(-1), mode='drop').reshape(TOKENS, NB)
    pair_pick = jnp.zeros((pairs,), jnp.float32).at[target].set(picks.reshape(-1), mode='drop').reshape(TOKENS, NB)
    top = lax.optimization_barrier(jnp.max(pair_peak, axis=1))
    summed = lax.optimization_barrier(jnp.sum(pair_total * jnp.exp(pair_peak - top[:, None]), axis=1))
    chosen = lax.optimization_barrier(jnp.sum(pair_pick, axis=1))
    return chosen - top - jnp.log(summed)
```

```python
import jax
import jax.numpy as jnp
from jax import lax
from jax.sharding import Mesh
from jax.sharding import PartitionSpec as P

D = 8192
VB = 297
VP = 304
IMG = 64
CAP = 10
GROUP = 4

sharpness_divisor = 0.7
epsilon = 1e-06
floor_value = -1e30

SEQ = ("x", "z")
TEN = ("core", "y")


def exchange(value, axis):
    return lax.all_to_all(value, axis, split_axis=0, concat_axis=0, tiled=True)


def pack(scores):
    tail = scores[..., 256:]
    tail = jnp.concatenate([tail[..., : VP // 2, :], tail[..., VP // 2 :, :]], axis=-1)
    return jnp.concatenate([scores[..., :128], scores[..., 128:256], tail], axis=-2)


def unpack(packed):
    tail = packed[..., 2 * VP :, :]
    tail = jnp.concatenate([tail[..., :64], tail[..., 64:]], axis=-2)
    return jnp.concatenate([packed[..., :VP, :], packed[..., VP : 2 * VP, :], tail], axis=-1)


def per_device(text, patches, norm_gain, head, image_rows, patch_owner, nucleus, code):
    del patch_owner
    shards = lax.axis_size(SEQ)
    columns = lax.axis_size(TEN)
    cores, chips = lax.axis_size("core"), lax.axis_size("y")
    y, core = lax.axis_index("y"), lax.axis_index("core")
    place = y * cores + core
    number = core * chips + y
    tokens, width = text.shape
    slots = tokens // IMG
    blocks = shards * columns
    members = shards * CAP

    pieces = head.reshape(VB, chips, cores, width).transpose(2, 1, 0, 3).reshape(columns, VB, width)
    head_here = exchange(pieces, TEN)

    both = jnp.concatenate([text, patches], axis=0)
    everyone = lax.all_gather(both, SEQ, axis=0, tiled=True)

    with jax.named_scope("routing"):
        ids = jnp.arange(blocks, dtype=jnp.int32)
        named = jnp.any(nucleus[:, :, None] == ids[None, None, :], axis=1)
        lower = (jnp.arange(tokens)[:, None] > jnp.arange(tokens)[None, :]).astype(jnp.bfloat16)
        rank = jnp.dot(lower, named.astype(jnp.bfloat16), preferred_element_type=jnp.float32).astype(jnp.int32)
        entry = jnp.arange(nucleus.shape[1], dtype=jnp.int32)
        target = jnp.sum(jnp.where(entry[None, :] == (code // VB)[:, None], nucleus, 0), axis=1)
        mark = jnp.where(target[:, None] == ids[None, :], (code % VB + 1)[:, None], 0)
        value = (jnp.arange(tokens, dtype=jnp.int32)[:, None] + 1) * 512 + mark
        rank = jnp.where(named, rank, -1)
        slot = jnp.arange(CAP, dtype=jnp.int32)
        lists = jnp.sum(jnp.where(rank[None] == slot[:, None, None], value[None], 0), axis=1)
        lists = lists.reshape(CAP, shards, chips, cores).transpose(1, 3, 2, 0).reshape(shards, columns, CAP)

    squares = jnp.sum(jnp.square(both.astype(jnp.float32)), axis=1)
    squares = lax.psum(squares, TEN)
    firsts = image_rows.reshape(slots, IMG)[:, 0].astype(jnp.float32)
    common = jnp.concatenate([squares, firsts])
    message = jnp.concatenate(
        [
            lists.reshape(shards, columns * CAP).astype(jnp.float32),
            jnp.broadcast_to(common[None, :], (shards, common.shape[0])),
        ],
        axis=1,
    )
    told = exchange(message, SEQ)
    told_lists = told[:, : columns * CAP].astype(jnp.int32).reshape(shards, columns, CAP)
    told_squares = told[:, columns * CAP : columns * CAP + 2 * tokens]
    told_firsts = told[:, columns * CAP + 2 * tokens :].astype(jnp.int32)

    with jax.named_scope("merge"):
        own_unit = jnp.arange(shards, dtype=jnp.int32)[:, None] * (2 * slots) + jnp.arange(slots, dtype=jnp.int32)[None, :]
        patch_unit = (told_firsts // tokens) * (2 * slots) + slots + (told_firsts % tokens) // IMG
        unit = jnp.where(told_firsts >= 0, patch_unit, own_unit).reshape(-1)
        pick = unit[:, None] == jnp.arange(shards * 2 * slots, dtype=jnp.int32)[None, :]
        units = everyone.reshape(shards * 2 * slots, IMG * width)
        merged = jnp.dot(pick.astype(jnp.bfloat16), units, preferred_element_type=jnp.float32)
        unit_squares = told_squares.reshape(1, shards * 2 * slots, IMG)
        row_squares = jnp.sum(jnp.where(pick[:, :, None], unit_squares, 0.0), axis=1)
        scale = lax.rsqrt(row_squares / D + epsilon)
        gain = lax.dynamic_slice_in_dim(norm_gain, place * width, width, 0)
        normed = (merged.reshape(shards * slots, IMG, width) * scale[:, :, None] * gain).astype(jnp.bfloat16)

    with jax.named_scope("partial"):
        groups = shards // GROUP
        token_of = told_lists // 512 - 1 + (jnp.arange(shards, dtype=jnp.int32) % GROUP * tokens)[:, None, None]
        token_of = jnp.where(told_lists > 0, token_of, -1)
        token_of = token_of.reshape(groups, GROUP, columns, CAP).transpose(0, 2, 1, 3).reshape(groups, columns * GROUP * CAP)
        hot = (token_of[:, :, None] == jnp.arange(GROUP * tokens, dtype=jnp.int32)).astype(jnp.bfloat16)
        rows = jnp.einsum(
            "gpt,gtk->gpk", hot, normed.reshape(groups, GROUP * tokens, width), preferred_element_type=jnp.float32
        ).astype(jnp.bfloat16)
        rows = rows.reshape(groups, columns, GROUP * CAP, width).transpose(1, 0, 2, 3).reshape(columns, members, width)
        partial = jnp.einsum("cvk,cpk->cvp", head_here, rows, preferred_element_type=jnp.float32)
        partial = jnp.pad(partial, ((0, 0), (0, VP - VB), (0, 0)))
        packed = pack(partial).astype(jnp.float16)

    packed = packed.reshape((cores, chips) + packed.shape[1:])
    halves = exchange(packed, "core")
    halves = jnp.sum(halves.astype(jnp.float32), axis=0).astype(jnp.float16)
    parts = exchange(halves, "y")
    scores = unpack(jnp.sum(parts.astype(jnp.float32), axis=0))[:VB] / sharpness_divisor

    with jax.named_scope("softmax"):
        mine = lax.dynamic_index_in_dim(told_lists, number, 1, keepdims=False).reshape(members)
        offset = mine % 512 - 1
        peak = jnp.max(scores, axis=0)
        total = jnp.sum(jnp.exp(scores - peak[None, :]), axis=0)
        entry_id = lax.broadcasted_iota(jnp.int32, scores.shape, 0)
        picked = jnp.sum(jnp.where(entry_id == offset[None, :], scores, 0.0), axis=0)
    answer = jnp.stack([peak, total, picked]).reshape(3, shards, CAP).transpose(1, 0, 2)
    answer = exchange(answer.reshape(shards, 3 * CAP), SEQ).reshape(shards, 3, CAP).transpose(1, 0, 2)
    peak, total, picked = answer.reshape(3, members)
    with jax.named_scope("combine"):
        sent = lax.dynamic_index_in_dim(lists, number, 1, keepdims=False).reshape(members)
        token = jnp.where(sent > 0, sent // 512 - 1, -1)
        member = token[:, None] == jnp.arange(tokens, dtype=jnp.int32)[None, :]
        local_peak = jnp.max(jnp.where(member, peak[:, None], floor_value), axis=0)
        scaled = jnp.exp(jnp.where(member, peak[:, None] - local_peak[None, :], floor_value))
        local_total = jnp.sum(scaled * total[:, None], axis=0)
        local_pick = jnp.sum(jnp.where(member, picked[:, None], 0.0), axis=0)
        local = jnp.stack([local_peak, local_total, local_pick])
    every = lax.all_gather(local, TEN, axis=0)
    top = jnp.max(every[:, 0], axis=0)
    summed = jnp.sum(every[:, 1] * jnp.exp(every[:, 0] - top[None, :]), axis=0)
    chosen = jnp.sum(every[:, 2], axis=0)
    return chosen - top - jnp.log(summed)


def solution(mesh):
    fine = Mesh(mesh.devices.reshape(4, 8, 8, 2), ("x", "z", "y", "core"))
    seq, tensor = ("x", "z"), ("y", "core")
    return jax.shard_map(
        per_device,
        mesh=fine,
        in_specs=(
            P(seq, tensor),
            P(seq, tensor),
            P(),
            P(seq + tensor, None),
            P(seq),
            P(seq),
            P(seq, None),
            P(seq),
        ),
        out_specs=P(seq),
        check_vma=False,
    )
```

```python
import jax
import jax.numpy as jnp
from jax import lax
from jax.experimental import pallas as pl
from jax.experimental.pallas import tpu as pltpu
from jax.sharding import Mesh
from jax.sharding import PartitionSpec as P

D = 8192
VB = 297
VP = 304
IMG = 64
CAP = 10
GROUP = 8
TALL = 760
VMEM = 48 * 2**20

sharpness_divisor = 0.7
epsilon = 1e-06
floor_value = -1e30

SEQ = ("x", "z")
TEN = ("core", "y")


def exchange(value, axis):
    return lax.all_to_all(value, axis, split_axis=0, concat_axis=0, tiled=True)


def share(value, axis):
    return exchange(jnp.broadcast_to(value[None], (lax.axis_size(axis),) + value.shape), axis)


def split_kernel(head_ref, out_ref):
    rows = lax.broadcasted_iota(jnp.int32, out_ref.shape[1:], 0)
    out_ref[0] = jnp.where(rows < VB, head_ref[...].astype(jnp.float32), 0.0).astype(jnp.bfloat16)


def split_head(head, chips, cores):
    width = head.shape[1] // (chips * cores)
    return pl.pallas_call(
        split_kernel,
        grid=(chips * cores,),
        in_specs=[pl.BlockSpec((VP, width), lambda i: (0, i % chips * cores + i // chips))],
        out_specs=pl.BlockSpec((1, VP, width), lambda i: (i, 0, 0)),
        out_shape=jax.ShapeDtypeStruct((chips * cores, VP, width), jnp.bfloat16),
        compiler_params=pltpu.CompilerParams(vmem_limit_bytes=VMEM),
        name="split_head",
    )(head)


def rows_kernel(unit_ref, *refs):
    del unit_ref
    *pieces, scale_ref, gain_ref, token_ref, out_ref, normed_ref = refs
    for i, piece in enumerate(pieces):
        here = pl.ds(i * IMG, IMG)
        values = piece[...].astype(jnp.float32)
        normed_ref[here, :] = (values * scale_ref[here, :] * gain_ref[...]).astype(jnp.bfloat16)
    token = token_ref[0]
    shape = (token.shape[0], normed_ref.shape[0])
    hot = (token == lax.broadcasted_iota(jnp.int32, shape, 1)).astype(jnp.float32).astype(jnp.bfloat16)
    rows = jnp.dot(hot, normed_ref[...], preferred_element_type=jnp.float32)
    out_ref[...] = rows.astype(jnp.bfloat16).reshape(out_ref.shape)


def pick_rows(unit, everyone, scale, gain, token_of, columns):
    groups, pairs, _ = token_of.shape
    width = everyone.shape[1]
    units = unit.shape[0] // groups
    piece = [
        pl.BlockSpec((IMG, width), lambda g, unit_ref, i=i: (unit_ref[g * units + i], 0)) for i in range(units)
    ]
    return pl.pallas_call(
        rows_kernel,
        grid_spec=pltpu.PrefetchScalarGridSpec(
            num_scalar_prefetch=1,
            grid=(groups,),
            in_specs=piece
            + [
                pl.BlockSpec((units * IMG, 1), lambda g, unit_ref: (g, 0)),
                pl.BlockSpec((1, width), lambda g, unit_ref: (0, 0)),
                pl.BlockSpec((1, pairs, 1), lambda g, unit_ref: (g, 0, 0)),
            ],
            out_specs=pl.BlockSpec((columns, pairs // columns, width), lambda g, unit_ref: (0, g, 0)),
            scratch_shapes=[pltpu.VMEM((units * IMG, width), jnp.bfloat16)],
        ),
        out_shape=jax.ShapeDtypeStruct((columns, groups * pairs // columns, width), jnp.bfloat16),
        compiler_params=pltpu.CompilerParams(vmem_limit_bytes=VMEM),
        cost_estimate=pl.CostEstimate(flops=1000, bytes_accessed=1000, transcendentals=0),
        name="pick_rows",
    )(unit, *([everyone] * units), scale, gain, token_of)


def partial_kernel(head_ref, rows_ref, out_ref):
    scores = lax.dot_general(
        head_ref[0], rows_ref[0], (((1,), (1,)), ((), ())), preferred_element_type=jnp.float32
    )
    half = VP // 2
    tail = jnp.concatenate([scores[:half, 256:320], scores[half:, 256:320]], axis=1)
    out_ref[0, :VP, :] = scores[:, :128].astype(out_ref.dtype)
    out_ref[0, VP : 2 * VP, :] = scores[:, 128:256].astype(out_ref.dtype)
    out_ref[0, 2 * VP :, :] = tail.astype(out_ref.dtype)


def partial_scores(head, rows):
    columns, _, width = head.shape
    return pl.pallas_call(
        partial_kernel,
        grid=(columns,),
        in_specs=[
            pl.BlockSpec((1, VP, width), lambda i: (i, 0, 0)),
            pl.BlockSpec((1, rows.shape[1], width), lambda i: (i, 0, 0)),
        ],
        out_specs=pl.BlockSpec((1, TALL, 128), lambda i: (i, 0, 0)),
        out_shape=jax.ShapeDtypeStruct((columns, TALL, 128), jnp.float32),
        compiler_params=pltpu.CompilerParams(vmem_limit_bytes=VMEM),
        name="partial_scores",
    )(head, rows)


def unpack(packed):
    tail = packed[..., 2 * VP :, :]
    tail = jnp.concatenate([tail[..., :64], tail[..., 64:]], axis=-2)
    return jnp.concatenate([packed[..., :VP, :], packed[..., VP : 2 * VP, :], tail], axis=-1)


def per_device(text, patches, norm_gain, head, image_rows, patch_owner, nucleus, code):
    del patch_owner
    shards = lax.axis_size(SEQ)
    columns = lax.axis_size(TEN)
    cores, chips = lax.axis_size("core"), lax.axis_size("y")
    y, core = lax.axis_index("y"), lax.axis_index("core")
    place = y * cores + core
    number = core * chips + y
    tokens, width = text.shape
    slots = tokens // IMG
    blocks = shards * columns
    members = shards * CAP

    pieces = split_head(head, chips, cores)
    both = jnp.concatenate([text, patches], axis=0)
    everyone = lax.all_gather(both, SEQ, axis=0, tiled=True)

    with jax.named_scope("routing"):
        ids = jnp.arange(blocks, dtype=jnp.int32)
        named = jnp.any(nucleus[:, :, None] == ids[None, None, :], axis=1)
        lower = (jnp.arange(tokens)[:, None] > jnp.arange(tokens)[None, :]).astype(jnp.bfloat16)
        rank = jnp.dot(lower, named.astype(jnp.bfloat16), preferred_element_type=jnp.float32).astype(jnp.int32)
        entry = jnp.arange(nucleus.shape[1], dtype=jnp.int32)
        target = jnp.sum(jnp.where(entry[None, :] == (code // VB)[:, None], nucleus, 0), axis=1)
        mark = jnp.where(target[:, None] == ids[None, :], (code % VB + 1)[:, None], 0)
        value = (jnp.arange(tokens, dtype=jnp.int32)[:, None] + 1) * 512 + mark
        rank = jnp.where(named, rank, -1)
        slot = jnp.arange(CAP, dtype=jnp.int32)
        lists = jnp.sum(jnp.where(rank[None] == slot[:, None, None], value[None], 0), axis=1)
        lists = lists.reshape(CAP, shards, chips, cores).transpose(1, 3, 2, 0).reshape(shards, columns, CAP)

    squares = jnp.sum(jnp.square(both.astype(jnp.float32)), axis=1)
    firsts = image_rows.reshape(slots, IMG)[:, 0].astype(jnp.float32)
    common = jnp.concatenate([squares, firsts])
    message = jnp.concatenate(
        [
            lists.reshape(shards, columns * CAP).astype(jnp.float32),
            jnp.broadcast_to(common[None, :], (shards, common.shape[0])),
        ],
        axis=1,
    )
    told = exchange(message, SEQ)
    told, pieces = lax.optimization_barrier((told, pieces))
    head_here = exchange(pieces, TEN)
    told_lists = told[:, : columns * CAP].astype(jnp.int32).reshape(shards, columns, CAP)
    told_squares = told[:, columns * CAP : columns * CAP + 2 * tokens]
    told_firsts = told[:, columns * CAP + 2 * tokens :].astype(jnp.int32)

    with jax.named_scope("merge"):
        own_unit = jnp.arange(shards, dtype=jnp.int32)[:, None] * (2 * slots) + jnp.arange(slots, dtype=jnp.int32)[None, :]
        patch_unit = (told_firsts // tokens) * (2 * slots) + slots + (told_firsts % tokens) // IMG
        unit = jnp.where(told_firsts >= 0, patch_unit, own_unit).reshape(-1)
        pick = unit[:, None] == jnp.arange(shards * 2 * slots, dtype=jnp.int32)[None, :]
        unit_squares = told_squares.reshape(1, shards * 2 * slots, IMG)
        row_squares = jnp.sum(jnp.where(pick[:, :, None], unit_squares, 0.0), axis=1)
        row_squares = lax.psum(row_squares, TEN)
        scale = lax.rsqrt(row_squares / D + epsilon)
        gain = lax.dynamic_slice_in_dim(norm_gain, place * width, width, 0)

    with jax.named_scope("partial"):
        groups = shards // GROUP
        token_of = told_lists // 512 - 1 + (jnp.arange(shards, dtype=jnp.int32) % GROUP * tokens)[:, None, None]
        token_of = jnp.where(told_lists > 0, token_of, -1)
        token_of = token_of.reshape(groups, GROUP, columns, CAP).transpose(0, 2, 1, 3)
        token_of = token_of.reshape(groups, columns * GROUP * CAP, 1)
        rows = pick_rows(unit, everyone, scale.reshape(-1, 1), gain[None, :], token_of, columns)
        packed = partial_scores(head_here, rows)

    packed = packed.reshape((cores, chips) + packed.shape[1:])
    halves = exchange(packed, "core")
    halves = jnp.sum(halves, axis=0).astype(jnp.float16)
    parts = exchange(halves, "y")
    scores = unpack(jnp.sum(parts.astype(jnp.float32), axis=0))[:VB] / sharpness_divisor

    with jax.named_scope("softmax"):
        mine = lax.dynamic_index_in_dim(told_lists, number, 1, keepdims=False).reshape(members)
        offset = mine % 512 - 1
        peak = jnp.max(scores, axis=0)
        total = jnp.sum(jnp.exp(scores - peak[None, :]), axis=0)
        entry_id = lax.broadcasted_iota(jnp.int32, scores.shape, 0)
        picked = jnp.sum(jnp.where(entry_id == offset[None, :], scores, 0.0), axis=0)
    answer = jnp.stack([peak, total, picked]).reshape(3, shards, CAP).transpose(1, 0, 2)
    answer = exchange(answer.reshape(shards, 3 * CAP), SEQ).reshape(shards, 3, CAP).transpose(1, 0, 2)
    peak, total, picked = answer.reshape(3, members)
    with jax.named_scope("combine"):
        sent = lax.dynamic_index_in_dim(lists, number, 1, keepdims=False).reshape(members)
        token = jnp.where(sent > 0, sent // 512 - 1, -1)
        member = token[:, None] == jnp.arange(tokens, dtype=jnp.int32)[None, :]
        local_peak = jnp.max(jnp.where(member, peak[:, None], floor_value), axis=0)
        scaled = jnp.exp(jnp.where(member, peak[:, None] - local_peak[None, :], floor_value))
        local_total = jnp.sum(scaled * total[:, None], axis=0)
        local_pick = jnp.sum(jnp.where(member, picked[:, None], 0.0), axis=0)
        local = jnp.stack([local_peak, local_total, local_pick])
    every = share(local, TEN)
    top = jnp.max(every[:, 0], axis=0)
    summed = jnp.sum(every[:, 1] * jnp.exp(every[:, 0] - top[None, :]), axis=0)
    chosen = jnp.sum(every[:, 2], axis=0)
    return chosen - top - jnp.log(summed)


def solution(mesh):
    fine = Mesh(mesh.devices.reshape(4, 8, 8, 2), ("x", "z", "y", "core"))
    seq, tensor = ("x", "z"), ("y", "core")
    return jax.shard_map(
        per_device,
        mesh=fine,
        in_specs=(
            P(seq, tensor),
            P(seq, tensor),
            P(),
            P(seq + tensor, None),
            P(seq),
            P(seq),
            P(seq, None),
            P(seq),
        ),
        out_specs=P(seq),
        check_vma=False,
    )
```

```python
import jax
import jax.numpy as jnp
from jax import lax
from jax.experimental import pallas as pl
from jax.experimental.pallas import tpu as pltpu
from jax.sharding import Mesh
from jax.sharding import PartitionSpec as P

D = 8192
VB = 297
VP = 304
IMG = 64
CAP = 10
GROUP = 8
TALL = 760
VMEM = 60 * 2**20

sharpness_divisor = 0.7
epsilon = 1e-06
floor_value = -1e30

SEQ = ("x", "z")
TEN = ("core", "y")


def exchange(value, axis):
    return lax.all_to_all(value, axis, split_axis=0, concat_axis=0, tiled=True)


def share(value, axis):
    return exchange(jnp.broadcast_to(value[None], (lax.axis_size(axis),) + value.shape), axis)


def by_steps(value, axis):
    count, me = lax.axis_size(axis), lax.axis_index(axis)
    twice = jnp.concatenate([value, value], axis=0)
    turned = lax.dynamic_slice_in_dim(twice, me, count, 0)
    came = [turned[0]]
    for step in range(1, count):
        came.append(lax.ppermute(turned[step], axis, [(i, (i + step) % count) for i in range(count)]))
    back = jnp.stack(came[::-1])
    twice = jnp.concatenate([back, back], axis=0)
    return lax.dynamic_slice_in_dim(twice, count - 1 - me, count, 0)


def split_kernel(head_ref, out_ref):
    rows = lax.broadcasted_iota(jnp.int32, out_ref.shape[1:], 0)
    out_ref[0] = jnp.where(rows < VB, head_ref[...].astype(jnp.float32), 0.0).astype(jnp.bfloat16)


def split_head(head, chips):
    part = head.shape[1] // chips
    return pl.pallas_call(
        split_kernel,
        grid=(chips,),
        in_specs=[pl.BlockSpec((VP, part), lambda i: (0, i))],
        out_specs=pl.BlockSpec((1, VP, part), lambda i: (i, 0, 0)),
        out_shape=jax.ShapeDtypeStruct((chips, VP, part), jnp.bfloat16),
        compiler_params=pltpu.CompilerParams(vmem_limit_bytes=VMEM),
        name="split_head",
    )(head)


def rows_kernel(unit_ref, *refs):
    del unit_ref
    *pieces, scale_ref, gain_ref, token_ref, away_ref, here_ref, normed_ref = refs
    for i, piece in enumerate(pieces):
        span = pl.ds(i * IMG, IMG)
        values = piece[...].astype(jnp.float32)
        normed_ref[span, :] = (values * scale_ref[span, :] * gain_ref[...]).astype(jnp.bfloat16)
    token = token_ref[0]
    half = token.shape[0] // 2
    for part, out_ref in enumerate((away_ref, here_ref)):
        wanted = token[part * half : (part + 1) * half]
        shape = (half, normed_ref.shape[0])
        hot = (wanted == lax.broadcasted_iota(jnp.int32, shape, 1)).astype(jnp.float32).astype(jnp.bfloat16)
        rows = jnp.dot(hot, normed_ref[...], preferred_element_type=jnp.float32)
        out_ref[...] = rows.astype(jnp.bfloat16).reshape(out_ref.shape)


def pick_rows(unit, everyone, scale, gain, token_of, chips):
    groups, pairs, _ = token_of.shape
    width = everyone.shape[1]
    units = unit.shape[0] // groups
    each = pairs // (2 * chips)
    piece = [
        pl.BlockSpec((IMG, width), lambda g, unit_ref, i=i: (unit_ref[g * units + i], 0)) for i in range(units)
    ]
    return pl.pallas_call(
        rows_kernel,
        grid_spec=pltpu.PrefetchScalarGridSpec(
            num_scalar_prefetch=1,
            grid=(groups,),
            in_specs=piece
            + [
                pl.BlockSpec((units * IMG, 1), lambda g, unit_ref: (g, 0)),
                pl.BlockSpec((1, width), lambda g, unit_ref: (0, 0)),
                pl.BlockSpec((1, pairs, 1), lambda g, unit_ref: (g, 0, 0)),
            ],
            out_specs=[pl.BlockSpec((chips, each, width), lambda g, unit_ref: (0, g, 0))] * 2,
            scratch_shapes=[pltpu.VMEM((units * IMG, width), jnp.bfloat16)],
        ),
        out_shape=[jax.ShapeDtypeStruct((chips, groups * each, width), jnp.bfloat16)] * 2,
        compiler_params=pltpu.CompilerParams(vmem_limit_bytes=VMEM),
        name="pick_rows",
    )(unit, *([everyone] * units), scale, gain, token_of)


def partial_kernel(core_ref, head_here_ref, head_away_ref, here_ref, came_ref, out_ref):
    del core_ref
    across = (((1,), (1,)), ((), ()))
    scores = lax.dot_general(head_here_ref[0], here_ref[0], across, preferred_element_type=jnp.float32)
    scores += lax.dot_general(head_away_ref[0], came_ref[0], across, preferred_element_type=jnp.float32)
    half = VP // 2
    tail = jnp.concatenate([scores[:half, 256:320], scores[half:, 256:320]], axis=1)
    out_ref[0, :VP, :] = scores[:, :128]
    out_ref[0, VP : 2 * VP, :] = scores[:, 128:256]
    out_ref[0, 2 * VP :, :] = tail


def partial_scores(core, head, here, came):
    chips = head.shape[0]
    members, width = here.shape[1:]
    return pl.pallas_call(
        partial_kernel,
        grid_spec=pltpu.PrefetchScalarGridSpec(
            num_scalar_prefetch=1,
            grid=(chips,),
            in_specs=[
                pl.BlockSpec((1, VP, width), lambda i, core_ref: (i, 0, core_ref[0])),
                pl.BlockSpec((1, VP, width), lambda i, core_ref: (i, 0, 1 - core_ref[0])),
                pl.BlockSpec((1, members, width), lambda i, core_ref: (i, 0, 0)),
                pl.BlockSpec((1, members, width), lambda i, core_ref: (i, 0, 0)),
            ],
            out_specs=pl.BlockSpec((1, TALL, 128), lambda i, core_ref: (i, 0, 0)),
        ),
        out_shape=jax.ShapeDtypeStruct((chips, TALL, 128), jnp.float32),
        compiler_params=pltpu.CompilerParams(vmem_limit_bytes=VMEM),
        name="partial_scores",
    )(core[None], head, head, here, came)


def unpack(packed):
    tail = packed[..., 2 * VP :, :]
    tail = jnp.concatenate([tail[..., :64], tail[..., 64:]], axis=-2)
    return jnp.concatenate([packed[..., :VP, :], packed[..., VP : 2 * VP, :], tail], axis=-1)


def per_device(text, patches, norm_gain, head, image_rows, patch_owner, nucleus, code):
    del patch_owner
    shards = lax.axis_size(SEQ)
    columns = lax.axis_size(TEN)
    cores, chips = lax.axis_size("core"), lax.axis_size("y")
    y, core = lax.axis_index("y"), lax.axis_index("core")
    place = y * cores + core
    number = core * chips + y
    tokens, width = text.shape
    slots = tokens // IMG
    blocks = shards * columns
    members = shards * CAP

    both = jnp.concatenate([text, patches], axis=0)
    everyone = lax.all_gather(both, SEQ, axis=0, tiled=True)
    squares = jnp.sum(share(jnp.sum(jnp.square(both.astype(jnp.float32)), axis=1), TEN), axis=0)

    pieces, squares = lax.optimization_barrier((split_head(head, chips), squares))
    head_here = exchange(pieces, "y")

    with jax.named_scope("routing"):
        ids = jnp.arange(blocks, dtype=jnp.int32)
        named = jnp.any(nucleus[:, :, None] == ids[None, None, :], axis=1)
        lower = (jnp.arange(tokens)[:, None] > jnp.arange(tokens)[None, :]).astype(jnp.bfloat16)
        rank = jnp.dot(lower, named.astype(jnp.bfloat16), preferred_element_type=jnp.float32).astype(jnp.int32)
        entry = jnp.arange(nucleus.shape[1], dtype=jnp.int32)
        target = jnp.sum(jnp.where(entry[None, :] == (code // VB)[:, None], nucleus, 0), axis=1)
        mark = jnp.where(target[:, None] == ids[None, :], (code % VB + 1)[:, None], 0)
        value = (jnp.arange(tokens, dtype=jnp.int32)[:, None] + 1) * 512 + mark
        rank = jnp.where(named, rank, -1)
        slot = jnp.arange(CAP, dtype=jnp.int32)
        lists = jnp.sum(jnp.where(rank[None] == slot[:, None, None], value[None], 0), axis=1)
        lists = lists.reshape(CAP, shards, chips, cores).transpose(1, 3, 2, 0).reshape(shards, columns, CAP)

    firsts = image_rows.reshape(slots, IMG)[:, 0].astype(jnp.float32)
    common = jnp.concatenate([squares, firsts])
    message = jnp.concatenate(
        [
            lists.reshape(shards, columns * CAP).astype(jnp.float32),
            jnp.broadcast_to(common[None, :], (shards, common.shape[0])),
        ],
        axis=1,
    )
    told = by_steps(message.reshape(lax.axis_size("x"), lax.axis_size("z"), -1).swapaxes(0, 1), "z")
    told = by_steps(told.swapaxes(0, 1), "x").reshape(shards, -1)
    told_lists = told[:, : columns * CAP].astype(jnp.int32).reshape(shards, columns, CAP)
    told_squares = told[:, columns * CAP : columns * CAP + 2 * tokens]
    told_firsts = told[:, columns * CAP + 2 * tokens :].astype(jnp.int32)

    with jax.named_scope("merge"):
        own_unit = jnp.arange(shards, dtype=jnp.int32)[:, None] * (2 * slots) + jnp.arange(slots, dtype=jnp.int32)[None, :]
        patch_unit = (told_firsts // tokens) * (2 * slots) + slots + (told_firsts % tokens) // IMG
        unit = jnp.where(told_firsts >= 0, patch_unit, own_unit).reshape(-1)
        pick = unit[:, None] == jnp.arange(shards * 2 * slots, dtype=jnp.int32)[None, :]
        unit_squares = told_squares.reshape(1, shards * 2 * slots, IMG)
        row_squares = jnp.sum(jnp.where(pick[:, :, None], unit_squares, 0.0), axis=1)
        scale = lax.rsqrt(row_squares / D + epsilon)
        gain = lax.dynamic_slice_in_dim(norm_gain, place * width, width, 0)

    with jax.named_scope("partial"):
        groups = shards // GROUP
        token_of = told_lists // 512 - 1 + (jnp.arange(shards, dtype=jnp.int32) % GROUP * tokens)[:, None, None]
        token_of = jnp.where(told_lists > 0, token_of, -1)
        token_of = token_of.reshape(groups, GROUP, cores, chips, CAP).transpose(0, 2, 3, 1, 4)
        token_of = jnp.where(core == 0, token_of[:, ::-1], token_of)
        token_of = token_of.reshape(groups, columns * GROUP * CAP, 1)
        away, here = pick_rows(unit, everyone, scale.reshape(-1, 1), gain[None, :], token_of, chips)
        came = lax.ppermute(away, "core", [(0, 1), (1, 0)])
        packed = partial_scores(core, head_here, here, came).astype(jnp.float16)

    mine = lax.dynamic_index_in_dim(told_lists, number, 1, keepdims=False).reshape(members)
    offset = mine % 512 - 1
    sent = lax.dynamic_index_in_dim(lists, number, 1, keepdims=False).reshape(members)
    token = jnp.where(sent > 0, sent // 512 - 1, -1)
    packed, offset, token = lax.optimization_barrier((packed, offset, token))
    parts = exchange(packed, "y")
    scores = unpack(jnp.sum(parts.astype(jnp.float32), axis=0))[:VB] / sharpness_divisor

    with jax.named_scope("softmax"):
        peak = jnp.max(scores, axis=0)
        total = jnp.sum(jnp.exp(scores - peak[None, :]), axis=0)
        entry_id = lax.broadcasted_iota(jnp.int32, scores.shape, 0)
        picked = jnp.sum(jnp.where(entry_id == offset[None, :], scores, 0.0), axis=0)
    answer = jnp.stack([peak, total, picked]).reshape(3, shards, CAP).transpose(1, 0, 2)
    answer = exchange(answer.reshape(shards, 3 * CAP), SEQ).reshape(shards, 3, CAP).transpose(1, 0, 2)
    peak, total, picked = answer.reshape(3, members)
    with jax.named_scope("combine"):
        member = token[:, None] == jnp.arange(tokens, dtype=jnp.int32)[None, :]
        local_peak = jnp.max(jnp.where(member, peak[:, None], floor_value), axis=0)
        scaled = jnp.exp(jnp.where(member, peak[:, None] - local_peak[None, :], floor_value))
        local_total = jnp.sum(scaled * total[:, None], axis=0)
        local_pick = jnp.sum(jnp.where(member, picked[:, None], 0.0), axis=0)
        local = jnp.stack([local_peak, local_total, local_pick])
    every = share(local, TEN)
    top = jnp.max(every[:, 0], axis=0)
    summed = jnp.sum(every[:, 1] * jnp.exp(every[:, 0] - top[None, :]), axis=0)
    chosen = jnp.sum(every[:, 2], axis=0)
    return chosen - top - jnp.log(summed)


def solution(mesh):
    fine = Mesh(mesh.devices.reshape(4, 8, 8, 2), ("x", "z", "y", "core"))
    seq, tensor = ("x", "z"), ("y", "core")
    return jax.shard_map(
        per_device,
        mesh=fine,
        in_specs=(
            P(seq, tensor),
            P(seq, tensor),
            P(),
            P(seq + tensor, None),
            P(seq),
            P(seq),
            P(seq, None),
            P(seq),
        ),
        out_specs=P(seq),
        check_vma=False,
    )
```

```python
import jax
import jax.numpy as jnp
from jax import lax
from jax.experimental import pallas as pl
from jax.experimental.pallas import tpu as pltpu
from jax.sharding import Mesh
from jax.sharding import PartitionSpec as P

D = 8192
VB = 297
VP = 304
IMG = 64
CAP = 10
GROUP = 8
TALL = 760
STEPS = ((4, 3, 5), (2, 6, 1, 7, 0))
VMEM = 60 * 2**20

sharpness_divisor = 0.7
epsilon = 1e-06
floor_value = -1e30

SEQ = ("x", "z")
TEN = ("core", "y")


def exchange(value, axis):
    return lax.all_to_all(value, axis, split_axis=0, concat_axis=0, tiled=True)


def share(value, axis):
    return exchange(jnp.broadcast_to(value[None], (lax.axis_size(axis),) + value.shape), axis)


def by_steps(value, axis):
    count, me = lax.axis_size(axis), lax.axis_index(axis)
    twice = jnp.concatenate([value, value], axis=0)
    turned = lax.dynamic_slice_in_dim(twice, me, count, 0)
    came = [turned[0]]
    for step in range(1, count):
        came.append(lax.ppermute(turned[step], axis, [(i, (i + step) % count) for i in range(count)]))
    back = jnp.stack(came[::-1])
    twice = jnp.concatenate([back, back], axis=0)
    return lax.dynamic_slice_in_dim(twice, count - 1 - me, count, 0)


def front_kernel(text_ref, patches_ref, both_ref, squares_ref):
    tokens = text_ref.shape[0]
    for i, ref in enumerate((text_ref, patches_ref)):
        rows = ref[...]
        both_ref[pl.ds(i * tokens, tokens), :] = rows
        square = jnp.square(rows.astype(jnp.float32))
        square = sum(square[:, k : k + 128] for k in range(0, square.shape[1], 128))
        total = jnp.sum(square.T, axis=0, keepdims=True)
        squares_ref[:, i, :] = jnp.broadcast_to(total, (squares_ref.shape[0], tokens))


def front(text, patches, copies):
    tokens, width = text.shape
    return pl.pallas_call(
        front_kernel,
        out_shape=[
            jax.ShapeDtypeStruct((2 * tokens, width), jnp.bfloat16),
            jax.ShapeDtypeStruct((copies, 2, tokens), jnp.float32),
        ],
        name="front",
    )(text, patches)


def split_kernel(head_ref, out_ref):
    whole = VP - 16
    out_ref[0, :whole] = head_ref[:whole]
    last = head_ref[whole:].astype(jnp.float32)
    rows = lax.broadcasted_iota(jnp.int32, last.shape, 0) + whole
    out_ref[0, whole:] = jnp.where(rows < VB, last, 0.0).astype(jnp.bfloat16)


def split_head(head, chips):
    part = head.shape[1] // chips
    return pl.pallas_call(
        split_kernel,
        grid=(chips,),
        in_specs=[pl.BlockSpec((VP, part), lambda i: (0, i))],
        out_specs=pl.BlockSpec((1, VP, part), lambda i: (i, 0, 0)),
        out_shape=jax.ShapeDtypeStruct((chips, VP, part), jnp.bfloat16),
        compiler_params=pltpu.CompilerParams(vmem_limit_bytes=VMEM),
        name="split_head",
    )(head)


def column(row):
    return jnp.broadcast_to(row, (128, 128)).T


def rows_kernel(unit_ref, *refs):
    del unit_ref
    *pieces, scale_ref, gain_ref, token_ref, away_ref, here_ref, normed_ref, hot_ref = refs
    shards, tokens = scale_ref.shape[1:]
    per = tokens // IMG
    for shard in range(shards):
        scale = column(scale_ref[0, shard : shard + 1])
        scale = jnp.concatenate([scale] * (normed_ref.shape[1] // 128), axis=1)
        for slot in range(per):
            values = pieces[shard * per + slot][...].astype(jnp.float32)
            rows = values * scale[slot * IMG : (slot + 1) * IMG] * gain_ref[...]
            normed_ref[pl.ds(shard * tokens + slot * IMG, IMG), :] = rows.astype(jnp.bfloat16)
    lane = lax.broadcasted_iota(jnp.int32, (128, 128), 1)
    for chunk in range(token_ref.shape[1]):
        token = column(token_ref[0, chunk : chunk + 1])
        for shard in range(shards):
            hot = (token == lane + shard * tokens).astype(jnp.float32).astype(jnp.bfloat16)
            hot_ref[pl.ds(chunk * 128, 128), pl.ds(shard * tokens, tokens)] = hot
    half = hot_ref.shape[0] // 2
    for part, out_ref in enumerate((away_ref, here_ref)):
        rows = jnp.dot(hot_ref[pl.ds(part * half, half), :], normed_ref[...], preferred_element_type=jnp.float32)
        out_ref[...] = rows.astype(jnp.bfloat16).reshape(out_ref.shape)


def pick_rows(unit, everyone, scale, gain, token_of, chips):
    groups, chunks, _ = token_of.shape
    pairs = chunks * 128
    width = everyone.shape[1]
    units = unit.shape[0] // groups
    each = pairs // (2 * chips)
    piece = [
        pl.BlockSpec((IMG, width), lambda g, unit_ref, i=i: (unit_ref[g * units + i], 0)) for i in range(units)
    ]
    return pl.pallas_call(
        rows_kernel,
        grid_spec=pltpu.PrefetchScalarGridSpec(
            num_scalar_prefetch=1,
            grid=(groups,),
            in_specs=piece
            + [
                pl.BlockSpec((1,) + scale.shape[1:], lambda g, unit_ref: (g, 0, 0)),
                pl.BlockSpec((1, width), lambda g, unit_ref: (0, 0)),
                pl.BlockSpec((1, chunks, 128), lambda g, unit_ref: (g, 0, 0)),
            ],
            out_specs=[pl.BlockSpec((chips, each, width), lambda g, unit_ref: (0, g, 0))] * 2,
            scratch_shapes=[
                pltpu.VMEM((units * IMG, width), jnp.bfloat16),
                pltpu.VMEM((pairs, units * IMG), jnp.bfloat16),
            ],
        ),
        out_shape=[jax.ShapeDtypeStruct((chips, groups * each, width), jnp.bfloat16)] * 2,
        compiler_params=pltpu.CompilerParams(vmem_limit_bytes=56 * 2**20),
        name="pick_rows",
    )(unit, *([everyone] * units), scale, gain, token_of)


def partial_kernel(order_ref, head_here_ref, head_away_ref, here_ref, came_ref, out_ref):
    del order_ref
    across = (((1,), (1,)), ((), ()))
    scores = lax.dot_general(head_here_ref[0], here_ref[0], across, preferred_element_type=jnp.float32)
    scores += lax.dot_general(head_away_ref[0], came_ref[0], across, preferred_element_type=jnp.float32)
    half = VP // 2
    tail = jnp.concatenate([scores[:half, 256:320], scores[half:, 256:320]], axis=1)
    out_ref[0, :VP, :] = scores[:, :128]
    out_ref[0, VP : 2 * VP, :] = scores[:, 128:256]
    out_ref[0, 2 * VP :, :] = tail


def partial_scores(core, order, head, here, came):
    chips = order.shape[0]
    order = jnp.append(order, core)
    members, width = here.shape[1:]
    return pl.pallas_call(
        partial_kernel,
        grid_spec=pltpu.PrefetchScalarGridSpec(
            num_scalar_prefetch=1,
            grid=(chips,),
            in_specs=[
                pl.BlockSpec((1, VP, width), lambda i, order_ref: (order_ref[i], 0, order_ref[chips])),
                pl.BlockSpec((1, VP, width), lambda i, order_ref: (order_ref[i], 0, 1 - order_ref[chips])),
                pl.BlockSpec((1, members, width), lambda i, order_ref: (order_ref[i], 0, 0)),
                pl.BlockSpec((1, members, width), lambda i, order_ref: (order_ref[i], 0, 0)),
            ],
            out_specs=pl.BlockSpec((1, TALL, 128), lambda i, order_ref: (i, 0, 0)),
        ),
        out_shape=jax.ShapeDtypeStruct((chips, TALL, 128), jnp.float32),
        compiler_params=pltpu.CompilerParams(vmem_limit_bytes=16 * 2**20),
        name="partial_scores",
    )(order, head, head, here, came)


def unpack(packed):
    tail = packed[..., 2 * VP :, :]
    tail = jnp.concatenate([tail[..., :64], tail[..., 64:]], axis=-2)
    return jnp.concatenate([packed[..., :VP, :], packed[..., VP : 2 * VP, :], tail], axis=-1)


def per_device(text, patches, norm_gain, head, image_rows, patch_owner, nucleus, code):
    del patch_owner
    shards = lax.axis_size(SEQ)
    columns = lax.axis_size(TEN)
    cores, chips = lax.axis_size("core"), lax.axis_size("y")
    y, core = lax.axis_index("y"), lax.axis_index("core")
    place = y * cores + core
    number = core * chips + y
    tokens, width = text.shape
    slots = tokens // IMG
    blocks = shards * columns
    members = shards * CAP

    both, squares = front(text, patches, columns)
    everyone = lax.all_gather(both, SEQ, axis=0, tiled=True)
    squares = jnp.sum(exchange(squares, TEN), axis=0).reshape(-1)

    pieces, squares, nucleus, code = lax.optimization_barrier((split_head(head, chips), squares, nucleus, code))
    head_here = exchange(pieces, "y")

    with jax.named_scope("routing"):
        ids = jnp.arange(blocks, dtype=jnp.int32)
        named = jnp.any(nucleus[:, :, None] == ids[None, None, :], axis=1)
        lower = (jnp.arange(tokens)[:, None] > jnp.arange(tokens)[None, :]).astype(jnp.bfloat16)
        rank = jnp.dot(lower, named.astype(jnp.bfloat16), preferred_element_type=jnp.float32).astype(jnp.int32)
        entry = jnp.arange(nucleus.shape[1], dtype=jnp.int32)
        target = jnp.sum(jnp.where(entry[None, :] == (code // VB)[:, None], nucleus, 0), axis=1)
        mark = jnp.where(target[:, None] == ids[None, :], (code % VB + 1)[:, None], 0)
        value = (jnp.arange(tokens, dtype=jnp.int32)[:, None] + 1) * 512 + mark
        rank = jnp.where(named, rank, -1)
        slot = jnp.arange(CAP, dtype=jnp.int32)
        lists = jnp.sum(jnp.where(rank[None] == slot[:, None, None], value[None], 0), axis=1)
        lists = lists.reshape(CAP, shards, chips, cores).transpose(1, 3, 2, 0).reshape(shards, columns, CAP)

    firsts = image_rows.reshape(slots, IMG)[:, 0].astype(jnp.float32)
    common = jnp.concatenate([squares, firsts])
    message = jnp.concatenate(
        [
            lists.reshape(shards, columns * CAP).astype(jnp.float32),
            jnp.broadcast_to(common[None, :], (shards, common.shape[0])),
        ],
        axis=1,
    )
    told = by_steps(message.reshape(lax.axis_size("x"), lax.axis_size("z"), -1).swapaxes(0, 1), "z")
    told = by_steps(told.swapaxes(0, 1), "x").reshape(shards, -1)
    told_lists = told[:, : columns * CAP].astype(jnp.int32).reshape(shards, columns, CAP)
    told_squares = told[:, columns * CAP : columns * CAP + 2 * tokens]
    told_firsts = told[:, columns * CAP + 2 * tokens :].astype(jnp.int32)

    with jax.named_scope("merge"):
        own_unit = jnp.arange(shards, dtype=jnp.int32)[:, None] * (2 * slots) + jnp.arange(slots, dtype=jnp.int32)[None, :]
        patch_unit = (told_firsts // tokens) * (2 * slots) + slots + (told_firsts % tokens) // IMG
        unit = jnp.where(told_firsts >= 0, patch_unit, own_unit).reshape(-1)
        pick = unit[:, None] == jnp.arange(shards * 2 * slots, dtype=jnp.int32)[None, :]
        unit_squares = told_squares.reshape(1, shards * 2 * slots, IMG)
        row_squares = jnp.sum(jnp.where(pick[:, :, None], unit_squares, 0.0), axis=1)
        scale = lax.rsqrt(row_squares / D + epsilon)
        gain = lax.dynamic_slice_in_dim(norm_gain, place * width, width, 0)

    with jax.named_scope("partial"):
        groups = shards // GROUP
        token_of = told_lists // 512 - 1 + (jnp.arange(shards, dtype=jnp.int32) % GROUP * tokens)[:, None, None]
        token_of = jnp.where(told_lists > 0, token_of, -1)
        token_of = token_of.reshape(groups, GROUP, cores, chips, CAP).transpose(0, 2, 3, 1, 4)
        token_of = jnp.where(core == 0, token_of[:, ::-1], token_of)
        token_of = token_of.reshape(groups, columns * GROUP * CAP // 128, 128)
        away, here = pick_rows(unit, everyone, scale.reshape(groups, GROUP, tokens), gain[None, :], token_of, chips)
        came = lax.ppermute(away, "core", [(0, 1), (1, 0)])
        packed = []
        for part in STEPS:
            order = (y + jnp.array(part, jnp.int32)) % chips
            packed.append(partial_scores(core, order, head_here, here, came))

    mine = lax.dynamic_index_in_dim(told_lists, number, 1, keepdims=False).reshape(members)
    offset = mine % 512 - 1
    sent = lax.dynamic_index_in_dim(lists, number, 1, keepdims=False).reshape(members)
    token = jnp.where(sent > 0, sent // 512 - 1, -1)
    total = 0.0
    for part, scores in zip(STEPS, packed):
        for i, step in enumerate(part):
            if step == 0:
                total += scores[i]
            else:
                sent_part = scores[i].astype(jnp.float16)
                total += lax.ppermute(sent_part, "y", [(k, (k + step) % 8) for k in range(8)]).astype(jnp.float32)
    scores = unpack(total)[:VB] / sharpness_divisor

    with jax.named_scope("softmax"):
        peak = jnp.max(scores, axis=0)
        total = jnp.sum(jnp.exp(scores - peak[None, :]), axis=0)
        entry_id = lax.broadcasted_iota(jnp.int32, scores.shape, 0)
        picked = jnp.sum(jnp.where(entry_id == offset[None, :], scores, 0.0), axis=0)
    answer = jnp.stack([peak, total, picked]).reshape(3, shards, CAP).transpose(1, 0, 2)
    answer = exchange(answer.reshape(shards, 3 * CAP), SEQ).reshape(shards, 3, CAP).transpose(1, 0, 2)
    peak, total, picked = answer.reshape(3, members)
    with jax.named_scope("combine"):
        member = token[:, None] == jnp.arange(tokens, dtype=jnp.int32)[None, :]
        local_peak = jnp.max(jnp.where(member, peak[:, None], floor_value), axis=0)
        scaled = jnp.exp(jnp.where(member, peak[:, None] - local_peak[None, :], floor_value))
        local_total = jnp.sum(scaled * total[:, None], axis=0)
        local_pick = jnp.sum(jnp.where(member, picked[:, None], 0.0), axis=0)
        local = jnp.stack([local_peak, local_total, local_pick])
    every = share(local, TEN)
    top = jnp.max(every[:, 0], axis=0)
    summed = jnp.sum(every[:, 1] * jnp.exp(every[:, 0] - top[None, :]), axis=0)
    chosen = jnp.sum(every[:, 2], axis=0)
    return chosen - top - jnp.log(summed)


def solution(mesh):
    fine = Mesh(mesh.devices.reshape(4, 8, 8, 2), ("x", "z", "y", "core"))
    seq, tensor = ("x", "z"), ("y", "core")
    return jax.shard_map(
        per_device,
        mesh=fine,
        in_specs=(
            P(seq, tensor),
            P(seq, tensor),
            P(),
            P(seq + tensor, None),
            P(seq),
            P(seq),
            P(seq, None),
            P(seq),
        ),
        out_specs=P(seq),
        check_vma=False,
    )
```

```python
import jax
import jax.numpy as jnp
from jax import lax
from jax.experimental import pallas as pl
from jax.experimental.pallas import tpu as pltpu
from jax.sharding import Mesh
from jax.sharding import PartitionSpec as P

D = 8192
VB = 297
VP = 304
IMG = 64
CAP = 10
GROUP = 8
TALL = 760
STEPS = ((4,), (3, 5), (2, 6, 1, 7, 0))
VMEM = 60 * 2**20

sharpness_divisor = 0.7
epsilon = 1e-06
floor_value = -1e30

SEQ = ("x", "z")
TEN = ("core", "y")


def exchange(value, axis):
    return lax.all_to_all(value, axis, split_axis=0, concat_axis=0, tiled=True)


def share(value, axis):
    return exchange(jnp.broadcast_to(value[None], (lax.axis_size(axis),) + value.shape), axis)


def by_steps(value, axis):
    count, me = lax.axis_size(axis), lax.axis_index(axis)
    twice = jnp.concatenate([value, value], axis=0)
    turned = lax.dynamic_slice_in_dim(twice, me, count, 0)
    came = [turned[0]]
    for step in range(1, count):
        came.append(lax.ppermute(turned[step], axis, [(i, (i + step) % count) for i in range(count)]))
    back = jnp.stack(came[::-1])
    twice = jnp.concatenate([back, back], axis=0)
    return lax.dynamic_slice_in_dim(twice, count - 1 - me, count, 0)


def front_kernel(text_ref, patches_ref, both_ref, squares_ref):
    tokens = text_ref.shape[0]
    for i, ref in enumerate((text_ref, patches_ref)):
        rows = ref[...]
        both_ref[pl.ds(i * tokens, tokens), :] = rows
        square = jnp.square(rows.astype(jnp.float32))
        square = sum(square[:, k : k + 128] for k in range(0, square.shape[1], 128))
        total = jnp.sum(square.T, axis=0, keepdims=True)
        squares_ref[:, i, :] = jnp.broadcast_to(total, (squares_ref.shape[0], tokens))


def front(text, patches, copies):
    tokens, width = text.shape
    return pl.pallas_call(
        front_kernel,
        out_shape=[
            jax.ShapeDtypeStruct((2 * tokens, width), jnp.bfloat16),
            jax.ShapeDtypeStruct((copies, 2, tokens), jnp.float32),
        ],
        name="front",
    )(text, patches)


def split_kernel(head_ref, out_ref):
    whole = VP - 16
    out_ref[0, :whole] = head_ref[:whole]
    last = head_ref[whole:].astype(jnp.float32)
    blank = jnp.zeros((VP - VB, last.shape[1]), jnp.float32)
    out_ref[0, whole:] = jnp.concatenate([last, blank], axis=0).astype(jnp.bfloat16)


def split_head(head, chips):
    part = head.shape[1] // chips
    return pl.pallas_call(
        split_kernel,
        grid=(chips,),
        in_specs=[pl.BlockSpec((VB, part), lambda i: (0, i))],
        out_specs=pl.BlockSpec((1, VP, part), lambda i: (i, 0, 0)),
        out_shape=jax.ShapeDtypeStruct((chips, VP, part), jnp.bfloat16),
        compiler_params=pltpu.CompilerParams(vmem_limit_bytes=VMEM),
        name="split_head",
    )(head)


def column(row):
    return jnp.broadcast_to(row, (128, 128)).T


def rows_kernel(unit_ref, *refs):
    del unit_ref
    *pieces, scale_ref, gain_ref, token_ref, away_ref, here_ref, normed_ref, hot_ref = refs
    shards, tokens = scale_ref.shape[1:]
    per = tokens // IMG
    for shard in range(shards):
        scale = column(scale_ref[0, shard : shard + 1])
        scale = jnp.concatenate([scale] * (normed_ref.shape[1] // 128), axis=1)
        for slot in range(per):
            values = pieces[shard * per + slot][...].astype(jnp.float32)
            rows = values * scale[slot * IMG : (slot + 1) * IMG] * gain_ref[...]
            normed_ref[pl.ds(shard * tokens + slot * IMG, IMG), :] = rows.astype(jnp.bfloat16)
    lane = lax.broadcasted_iota(jnp.int32, (128, 128), 1)
    for chunk in range(token_ref.shape[1]):
        token = column(token_ref[0, chunk : chunk + 1])
        for shard in range(shards):
            hot = (token == lane + shard * tokens).astype(jnp.float32).astype(jnp.bfloat16)
            hot_ref[pl.ds(chunk * 128, 128), pl.ds(shard * tokens, tokens)] = hot
    half = hot_ref.shape[0] // 2
    for part, out_ref in enumerate((away_ref, here_ref)):
        rows = jnp.dot(hot_ref[pl.ds(part * half, half), :], normed_ref[...], preferred_element_type=jnp.float32)
        out_ref[...] = rows.astype(jnp.bfloat16).reshape(out_ref.shape)


def pick_rows(unit, everyone, scale, gain, token_of, chips):
    groups, chunks, _ = token_of.shape
    pairs = chunks * 128
    width = everyone.shape[1]
    units = unit.shape[0] // groups
    each = pairs // (2 * chips)
    piece = [
        pl.BlockSpec((IMG, width), lambda g, unit_ref, i=i: (unit_ref[g * units + i], 0)) for i in range(units)
    ]
    return pl.pallas_call(
        rows_kernel,
        grid_spec=pltpu.PrefetchScalarGridSpec(
            num_scalar_prefetch=1,
            grid=(groups,),
            in_specs=piece
            + [
                pl.BlockSpec((1,) + scale.shape[1:], lambda g, unit_ref: (g, 0, 0)),
                pl.BlockSpec((1, width), lambda g, unit_ref: (0, 0)),
                pl.BlockSpec((1, chunks, 128), lambda g, unit_ref: (g, 0, 0)),
            ],
            out_specs=[pl.BlockSpec((chips, each, width), lambda g, unit_ref: (0, g, 0))] * 2,
            scratch_shapes=[
                pltpu.VMEM((units * IMG, width), jnp.bfloat16),
                pltpu.VMEM((pairs, units * IMG), jnp.bfloat16),
            ],
        ),
        out_shape=[jax.ShapeDtypeStruct((chips, groups * each, width), jnp.bfloat16)] * 2,
        compiler_params=pltpu.CompilerParams(vmem_limit_bytes=32 * 2**20),
        name="pick_rows",
    )(unit, *([everyone] * units), scale, gain, token_of)


def partial_kernel(order_ref, head_here_ref, head_away_ref, here_ref, came_ref, out_ref):
    del order_ref
    across = (((1,), (1,)), ((), ()))
    scores = lax.dot_general(head_here_ref[0], here_ref[0], across, preferred_element_type=jnp.float32)
    scores += lax.dot_general(head_away_ref[0], came_ref[0], across, preferred_element_type=jnp.float32)
    half = VP // 2
    tail = jnp.concatenate([scores[:half, 256:320], scores[half:, 256:320]], axis=1)
    out_ref[0, :VP, :] = scores[:, :128]
    out_ref[0, VP : 2 * VP, :] = scores[:, 128:256]
    out_ref[0, 2 * VP :, :] = tail


def partial_scores(core, order, head, here, came):
    chips = order.shape[0]
    order = jnp.append(order, core)
    members, width = here.shape[1:]
    return pl.pallas_call(
        partial_kernel,
        grid_spec=pltpu.PrefetchScalarGridSpec(
            num_scalar_prefetch=1,
            grid=(chips,),
            in_specs=[
                pl.BlockSpec((1, VP, width), lambda i, order_ref: (order_ref[i], 0, order_ref[chips])),
                pl.BlockSpec((1, VP, width), lambda i, order_ref: (order_ref[i], 0, 1 - order_ref[chips])),
                pl.BlockSpec((1, members, width), lambda i, order_ref: (order_ref[i], 0, 0)),
                pl.BlockSpec((1, members, width), lambda i, order_ref: (order_ref[i], 0, 0)),
            ],
            out_specs=pl.BlockSpec((1, TALL, 128), lambda i, order_ref: (i, 0, 0)),
        ),
        out_shape=jax.ShapeDtypeStruct((chips, TALL, 128), jnp.float32),
        compiler_params=pltpu.CompilerParams(vmem_limit_bytes=16 * 2**20),
        name="partial_scores",
    )(order, head, head, here, came)


def unpack(packed):
    tail = packed[..., 2 * VP :, :]
    tail = jnp.concatenate([tail[..., :64], tail[..., 64:]], axis=-2)
    return jnp.concatenate([packed[..., :VP, :], packed[..., VP : 2 * VP, :], tail], axis=-1)


def per_device(text, patches, norm_gain, head, image_rows, patch_owner, nucleus, code):
    del patch_owner
    shards = lax.axis_size(SEQ)
    columns = lax.axis_size(TEN)
    cores, chips = lax.axis_size("core"), lax.axis_size("y")
    y, core = lax.axis_index("y"), lax.axis_index("core")
    place = y * cores + core
    number = core * chips + y
    tokens, width = text.shape
    slots = tokens // IMG
    blocks = shards * columns
    members = shards * CAP

    both, squares = front(text, patches, columns)
    everyone = lax.all_gather(both, SEQ, axis=0, tiled=True)
    squares = jnp.sum(exchange(squares, TEN), axis=0).reshape(-1)

    pieces, squares, nucleus, code = lax.optimization_barrier((split_head(head, chips), squares, nucleus, code))
    head_here = exchange(pieces, "y")

    with jax.named_scope("routing"):
        ids = jnp.arange(blocks, dtype=jnp.int32)
        named = jnp.any(nucleus[:, :, None] == ids[None, None, :], axis=1)
        lower = (jnp.arange(tokens)[:, None] > jnp.arange(tokens)[None, :]).astype(jnp.bfloat16)
        rank = jnp.dot(lower, named.astype(jnp.bfloat16), preferred_element_type=jnp.float32).astype(jnp.int32)
        entry = jnp.arange(nucleus.shape[1], dtype=jnp.int32)
        target = jnp.sum(jnp.where(entry[None, :] == (code // VB)[:, None], nucleus, 0), axis=1)
        mark = jnp.where(target[:, None] == ids[None, :], (code % VB + 1)[:, None], 0)
        value = (jnp.arange(tokens, dtype=jnp.int32)[:, None] + 1) * 512 + mark
        rank = jnp.where(named, rank, -1)
        slot = jnp.arange(CAP, dtype=jnp.int32)
        lists = jnp.sum(jnp.where(rank[None] == slot[:, None, None], value[None], 0), axis=1)
        lists = lists.reshape(CAP, shards, chips, cores).transpose(1, 3, 2, 0).reshape(shards, columns, CAP)

    firsts = image_rows.reshape(slots, IMG)[:, 0].astype(jnp.float32)
    common = jnp.concatenate([squares, firsts])
    message = jnp.concatenate(
        [
            lists.reshape(shards, columns * CAP).astype(jnp.float32),
            jnp.broadcast_to(common[None, :], (shards, common.shape[0])),
        ],
        axis=1,
    )
    told = by_steps(message.reshape(lax.axis_size("x"), lax.axis_size("z"), -1).swapaxes(0, 1), "z")
    told = by_steps(told.swapaxes(0, 1), "x").reshape(shards, -1)
    told_lists = told[:, : columns * CAP].astype(jnp.int32).reshape(shards, columns, CAP)
    told_squares = told[:, columns * CAP : columns * CAP + 2 * tokens]
    told_firsts = told[:, columns * CAP + 2 * tokens :].astype(jnp.int32)

    with jax.named_scope("merge"):
        own_unit = jnp.arange(shards, dtype=jnp.int32)[:, None] * (2 * slots) + jnp.arange(slots, dtype=jnp.int32)[None, :]
        patch_unit = (told_firsts // tokens) * (2 * slots) + slots + (told_firsts % tokens) // IMG
        unit = jnp.where(told_firsts >= 0, patch_unit, own_unit).reshape(-1)
        pick = unit[:, None] == jnp.arange(shards * 2 * slots, dtype=jnp.int32)[None, :]
        unit_squares = told_squares.reshape(1, shards * 2 * slots, IMG)
        row_squares = jnp.sum(jnp.where(pick[:, :, None], unit_squares, 0.0), axis=1)
        scale = lax.rsqrt(row_squares / D + epsilon)
        gain = lax.dynamic_slice_in_dim(norm_gain, place * width, width, 0)

    with jax.named_scope("partial"):
        groups = shards // GROUP
        token_of = told_lists // 512 - 1 + (jnp.arange(shards, dtype=jnp.int32) % GROUP * tokens)[:, None, None]
        token_of = jnp.where(told_lists > 0, token_of, -1)
        token_of = token_of.reshape(groups, GROUP, cores, chips, CAP).transpose(0, 2, 3, 1, 4)
        token_of = jnp.where(core == 0, token_of[:, ::-1], token_of)
        token_of = token_of.reshape(groups, columns * GROUP * CAP // 128, 128)
        away, here = pick_rows(unit, everyone, scale.reshape(groups, GROUP, tokens), gain[None, :], token_of, chips)
        came = lax.ppermute(away, "core", [(0, 1), (1, 0)])
        packed = []
        for part in STEPS:
            order = (y + jnp.array(part, jnp.int32)) % chips
            packed.append(partial_scores(core, order, head_here, here, came))

    mine = lax.dynamic_index_in_dim(told_lists, number, 1, keepdims=False).reshape(members)
    offset = mine % 512 - 1
    sent = lax.dynamic_index_in_dim(lists, number, 1, keepdims=False).reshape(members)
    token = jnp.where(sent > 0, sent // 512 - 1, -1)
    total = 0.0
    for part, scores in zip(STEPS, packed):
        for i, step in enumerate(part):
            if step == 0:
                total += scores[i]
            else:
                sent_part = scores[i].astype(jnp.float16)
                total += lax.ppermute(sent_part, "y", [(k, (k + step) % 8) for k in range(8)]).astype(jnp.float32)
    scores = unpack(total)[:VB] / sharpness_divisor

    with jax.named_scope("softmax"):
        peak = jnp.max(scores, axis=0)
        total = jnp.sum(jnp.exp(scores - peak[None, :]), axis=0)
        entry_id = lax.broadcasted_iota(jnp.int32, scores.shape, 0)
        picked = jnp.sum(jnp.where(entry_id == offset[None, :], scores, 0.0), axis=0)
    answer = jnp.stack([peak, total, picked]).reshape(3, shards, CAP).transpose(1, 0, 2)
    answer = exchange(answer.reshape(shards, 3 * CAP), SEQ).reshape(shards, 3, CAP).transpose(1, 0, 2)
    peak, total, picked = answer.reshape(3, members)
    with jax.named_scope("combine"):
        member = token[:, None] == jnp.arange(tokens, dtype=jnp.int32)[None, :]
        local_peak = jnp.max(jnp.where(member, peak[:, None], floor_value), axis=0)
        scaled = jnp.exp(jnp.where(member, peak[:, None] - local_peak[None, :], floor_value))
        local_total = jnp.sum(scaled * total[:, None], axis=0)
        local_pick = jnp.sum(jnp.where(member, picked[:, None], 0.0), axis=0)
        local = jnp.stack([local_peak, local_total, local_pick])
    every = share(local, TEN)
    top = jnp.max(every[:, 0], axis=0)
    summed = jnp.sum(every[:, 1] * jnp.exp(every[:, 0] - top[None, :]), axis=0)
    chosen = jnp.sum(every[:, 2], axis=0)
    return chosen - top - jnp.log(summed)


def solution(mesh):
    fine = Mesh(mesh.devices.reshape(4, 8, 8, 2), ("x", "z", "y", "core"))
    seq, tensor = ("x", "z"), ("y", "core")
    return jax.shard_map(
        per_device,
        mesh=fine,
        in_specs=(
            P(seq, tensor),
            P(seq, tensor),
            P(),
            P(seq + tensor, None),
            P(seq),
            P(seq),
            P(seq, None),
            P(seq),
        ),
        out_specs=P(seq),
        check_vma=False,
    )
```

```python
import jax
import jax.numpy as jnp
from jax import lax
from jax.experimental import pallas as pl
from jax.experimental.pallas import tpu as pltpu
from jax.sharding import Mesh
from jax.sharding import PartitionSpec as P

D = 8192
VB = 297
VP = 304
IMG = 64
CAP = 10
GROUP = 8
TALL = 760
STEPS = ((4, 3, 5), (2, 6, 1, 7, 0))
VMEM = 60 * 2**20

sharpness_divisor = 0.7
epsilon = 1e-06
floor_value = -1e30

SEQ = ("x", "z")
TEN = ("core", "y")


def exchange(value, axis):
    return lax.all_to_all(value, axis, split_axis=0, concat_axis=0, tiled=True)


def share(value, axis):
    return exchange(jnp.broadcast_to(value[None], (lax.axis_size(axis),) + value.shape), axis)


def by_steps(value, axis):
    count, me = lax.axis_size(axis), lax.axis_index(axis)
    twice = jnp.concatenate([value, value], axis=0)
    turned = lax.dynamic_slice_in_dim(twice, me, count, 0)
    came = [turned[0]]
    for step in range(1, count):
        came.append(lax.ppermute(turned[step], axis, [(i, (i + step) % count) for i in range(count)]))
    back = jnp.stack(came[::-1])
    twice = jnp.concatenate([back, back], axis=0)
    return lax.dynamic_slice_in_dim(twice, count - 1 - me, count, 0)


def front_kernel(text_ref, patches_ref, both_ref, squares_ref):
    tokens = text_ref.shape[0]
    for i, ref in enumerate((text_ref, patches_ref)):
        rows = ref[...]
        both_ref[pl.ds(i * tokens, tokens), :] = rows
        square = jnp.square(rows.astype(jnp.float32))
        square = sum(square[:, k : k + 128] for k in range(0, square.shape[1], 128))
        total = jnp.sum(square.T, axis=0, keepdims=True)
        squares_ref[:, i, :] = jnp.broadcast_to(total, (squares_ref.shape[0], tokens))


def front(text, patches, copies):
    tokens, width = text.shape
    return pl.pallas_call(
        front_kernel,
        out_shape=[
            jax.ShapeDtypeStruct((2 * tokens, width), jnp.bfloat16),
            jax.ShapeDtypeStruct((copies, 2, tokens), jnp.float32),
        ],
        name="front",
    )(text, patches)


def split_kernel(head_ref, out_ref):
    whole = VP - 16
    out_ref[0, :whole] = head_ref[:whole]
    last = head_ref[whole:].astype(jnp.float32)
    blank = jnp.zeros((VP - VB, last.shape[1]), jnp.float32)
    out_ref[0, whole:] = jnp.concatenate([last, blank], axis=0).astype(jnp.bfloat16)


def split_head(head, chips):
    part = head.shape[1] // chips
    return pl.pallas_call(
        split_kernel,
        grid=(chips,),
        in_specs=[pl.BlockSpec((VB, part), lambda i: (0, i))],
        out_specs=pl.BlockSpec((1, VP, part), lambda i: (i, 0, 0)),
        out_shape=jax.ShapeDtypeStruct((chips, VP, part), jnp.bfloat16),
        compiler_params=pltpu.CompilerParams(vmem_limit_bytes=VMEM),
        name="split_head",
    )(head)


def column(row):
    return jnp.broadcast_to(row, (128, 128)).T


def rows_kernel(unit_ref, *refs):
    del unit_ref
    *pieces, scale_ref, gain_ref, token_ref, away_ref, here_ref, normed_ref, hot_ref = refs
    shards, tokens = scale_ref.shape[1:]
    per = tokens // IMG
    for shard in range(shards):
        scale = column(scale_ref[0, shard : shard + 1])
        scale = jnp.concatenate([scale] * (normed_ref.shape[1] // 128), axis=1)
        for slot in range(per):
            values = pieces[shard * per + slot][...].astype(jnp.float32)
            rows = values * scale[slot * IMG : (slot + 1) * IMG] * gain_ref[...]
            normed_ref[pl.ds(shard * tokens + slot * IMG, IMG), :] = rows.astype(jnp.bfloat16)
    lane = lax.broadcasted_iota(jnp.int32, (128, 128), 1)
    for chunk in range(token_ref.shape[1]):
        token = column(token_ref[0, chunk : chunk + 1])
        for shard in range(shards):
            hot = (token == lane + shard * tokens).astype(jnp.float32).astype(jnp.bfloat16)
            hot_ref[pl.ds(chunk * 128, 128), pl.ds(shard * tokens, tokens)] = hot
    half = hot_ref.shape[0] // 2
    for part, out_ref in enumerate((away_ref, here_ref)):
        rows = jnp.dot(hot_ref[pl.ds(part * half, half), :], normed_ref[...], preferred_element_type=jnp.float32)
        out_ref[...] = rows.astype(jnp.bfloat16).reshape(out_ref.shape)


def pick_rows(unit, everyone, scale, gain, token_of, chips):
    groups, chunks, _ = token_of.shape
    pairs = chunks * 128
    width = everyone.shape[1]
    units = unit.shape[0] // groups
    each = pairs // (2 * chips)
    piece = [
        pl.BlockSpec((IMG, width), lambda g, unit_ref, i=i: (unit_ref[g * units + i], 0)) for i in range(units)
    ]
    return pl.pallas_call(
        rows_kernel,
        grid_spec=pltpu.PrefetchScalarGridSpec(
            num_scalar_prefetch=1,
            grid=(groups,),
            in_specs=piece
            + [
                pl.BlockSpec((1,) + scale.shape[1:], lambda g, unit_ref: (g, 0, 0)),
                pl.BlockSpec((1, width), lambda g, unit_ref: (0, 0)),
                pl.BlockSpec((1, chunks, 128), lambda g, unit_ref: (g, 0, 0)),
            ],
            out_specs=[pl.BlockSpec((chips, each, width), lambda g, unit_ref: (0, g, 0))] * 2,
            scratch_shapes=[
                pltpu.VMEM((units * IMG, width), jnp.bfloat16),
                pltpu.VMEM((pairs, units * IMG), jnp.bfloat16),
            ],
        ),
        out_shape=[jax.ShapeDtypeStruct((chips, groups * each, width), jnp.bfloat16)] * 2,
        compiler_params=pltpu.CompilerParams(vmem_limit_bytes=32 * 2**20),
        name="pick_rows",
    )(unit, *([everyone] * units), scale, gain, token_of)


def partial_kernel(order_ref, head_here_ref, head_away_ref, here_ref, came_ref, out_ref):
    del order_ref
    across = (((1,), (1,)), ((), ()))
    scores = lax.dot_general(head_here_ref[0], here_ref[0], across, preferred_element_type=jnp.float32)
    scores += lax.dot_general(head_away_ref[0], came_ref[0], across, preferred_element_type=jnp.float32)
    half = VP // 2
    tail = jnp.concatenate([scores[:half, 256:320], scores[half:, 256:320]], axis=1)
    out_ref[0, :VP, :] = scores[:, :128]
    out_ref[0, VP : 2 * VP, :] = scores[:, 128:256]
    out_ref[0, 2 * VP :, :] = tail


def partial_scores(core, order, head, here, came):
    chips = order.shape[0]
    order = jnp.append(order, core)
    members, width = here.shape[1:]
    return pl.pallas_call(
        partial_kernel,
        grid_spec=pltpu.PrefetchScalarGridSpec(
            num_scalar_prefetch=1,
            grid=(chips,),
            in_specs=[
                pl.BlockSpec((1, VP, width), lambda i, order_ref: (order_ref[i], 0, order_ref[chips])),
                pl.BlockSpec((1, VP, width), lambda i, order_ref: (order_ref[i], 0, 1 - order_ref[chips])),
                pl.BlockSpec((1, members, width), lambda i, order_ref: (order_ref[i], 0, 0)),
                pl.BlockSpec((1, members, width), lambda i, order_ref: (order_ref[i], 0, 0)),
            ],
            out_specs=pl.BlockSpec((1, TALL, 128), lambda i, order_ref: (i, 0, 0)),
        ),
        out_shape=jax.ShapeDtypeStruct((chips, TALL, 128), jnp.float32),
        compiler_params=pltpu.CompilerParams(vmem_limit_bytes=16 * 2**20),
        name="partial_scores",
    )(order, head, head, here, came)


def unpack(packed):
    tail = packed[..., 2 * VP :, :]
    tail = jnp.concatenate([tail[..., :64], tail[..., 64:]], axis=-2)
    return jnp.concatenate([packed[..., :VP, :], packed[..., VP : 2 * VP, :], tail], axis=-1)


def per_device(text, patches, norm_gain, head, image_rows, patch_owner, nucleus, code):
    del patch_owner
    shards = lax.axis_size(SEQ)
    columns = lax.axis_size(TEN)
    cores, chips = lax.axis_size("core"), lax.axis_size("y")
    y, core = lax.axis_index("y"), lax.axis_index("core")
    place = y * cores + core
    number = core * chips + y
    tokens, width = text.shape
    slots = tokens // IMG
    blocks = shards * columns
    members = shards * CAP

    both, squares = front(text, patches, columns)
    everyone = lax.all_gather(both, SEQ, axis=0, tiled=True)
    squares = jnp.sum(exchange(squares, TEN), axis=0).reshape(-1)

    pieces, squares, nucleus, code = lax.optimization_barrier((split_head(head, chips), squares, nucleus, code))
    head_here = exchange(pieces, "y")

    with jax.named_scope("routing"):
        ids = jnp.arange(blocks, dtype=jnp.int32)
        named = jnp.any(nucleus[:, :, None] == ids[None, None, :], axis=1)
        lower = (jnp.arange(tokens)[:, None] > jnp.arange(tokens)[None, :]).astype(jnp.bfloat16)
        rank = jnp.dot(lower, named.astype(jnp.bfloat16), preferred_element_type=jnp.float32).astype(jnp.int32)
        entry = jnp.arange(nucleus.shape[1], dtype=jnp.int32)
        target = jnp.sum(jnp.where(entry[None, :] == (code // VB)[:, None], nucleus, 0), axis=1)
        mark = jnp.where(target[:, None] == ids[None, :], (code % VB + 1)[:, None], 0)
        value = (jnp.arange(tokens, dtype=jnp.int32)[:, None] + 1) * 512 + mark
        rank = jnp.where(named, rank, -1)
        slot = jnp.arange(CAP, dtype=jnp.int32)
        lists = jnp.sum(jnp.where(rank[None] == slot[:, None, None], value[None], 0), axis=1)
        lists = lists.reshape(CAP, shards, chips, cores).transpose(1, 3, 2, 0).reshape(shards, columns, CAP)

    firsts = image_rows.reshape(slots, IMG)[:, 0].astype(jnp.float32)
    common = jnp.concatenate([squares, firsts])
    message = jnp.concatenate(
        [
            lists.reshape(shards, columns * CAP).astype(jnp.float32),
            jnp.broadcast_to(common[None, :], (shards, common.shape[0])),
        ],
        axis=1,
    )
    told = by_steps(message.reshape(lax.axis_size("x"), lax.axis_size("z"), -1).swapaxes(0, 1), "z")
    told = by_steps(told.swapaxes(0, 1), "x").reshape(shards, -1)
    told_lists = told[:, : columns * CAP].astype(jnp.int32).reshape(shards, columns, CAP)
    told_squares = told[:, columns * CAP : columns * CAP + 2 * tokens]
    told_firsts = told[:, columns * CAP + 2 * tokens :].astype(jnp.int32)

    with jax.named_scope("merge"):
        own_unit = jnp.arange(shards, dtype=jnp.int32)[:, None] * (2 * slots) + jnp.arange(slots, dtype=jnp.int32)[None, :]
        patch_unit = (told_firsts // tokens) * (2 * slots) + slots + (told_firsts % tokens) // IMG
        unit = jnp.where(told_firsts >= 0, patch_unit, own_unit).reshape(-1)
        pick = unit[:, None] == jnp.arange(shards * 2 * slots, dtype=jnp.int32)[None, :]
        unit_squares = told_squares.reshape(1, shards * 2 * slots, IMG)
        row_squares = jnp.sum(jnp.where(pick[:, :, None], unit_squares, 0.0), axis=1)
        scale = lax.rsqrt(row_squares / D + epsilon)
        gain = lax.dynamic_slice_in_dim(norm_gain, place * width, width, 0)

    with jax.named_scope("partial"):
        groups = shards // GROUP
        token_of = told_lists // 512 - 1 + (jnp.arange(shards, dtype=jnp.int32) % GROUP * tokens)[:, None, None]
        token_of = jnp.where(told_lists > 0, token_of, -1)
        token_of = token_of.reshape(groups, GROUP, cores, chips, CAP).transpose(0, 2, 3, 1, 4)
        token_of = jnp.where(core == 0, token_of[:, ::-1], token_of)
        token_of = token_of.reshape(groups, columns * GROUP * CAP // 128, 128)
        away, here = pick_rows(unit, everyone, scale.reshape(groups, GROUP, tokens), gain[None, :], token_of, chips)
        came = lax.ppermute(away, "core", [(0, 1), (1, 0)])
        packed = []
        for part in STEPS:
            order = (y + jnp.array(part, jnp.int32)) % chips
            packed.append(partial_scores(core, order, head_here, here, came))

    mine = lax.dynamic_index_in_dim(told_lists, number, 1, keepdims=False).reshape(members)
    offset = mine % 512 - 1
    sent = lax.dynamic_index_in_dim(lists, number, 1, keepdims=False).reshape(members)
    token = jnp.where(sent > 0, sent // 512 - 1, -1)
    total = 0.0
    for part, scores in zip(STEPS, packed):
        for i, step in enumerate(part):
            if step == 0:
                total += scores[i]
            else:
                sent_part = scores[i].astype(jnp.float16)
                total += lax.ppermute(sent_part, "y", [(k, (k + step) % 8) for k in range(8)]).astype(jnp.float32)
    scores = unpack(total)[:VB] / sharpness_divisor

    with jax.named_scope("softmax"):
        peak = jnp.max(scores, axis=0)
        total = jnp.sum(jnp.exp(scores - peak[None, :]), axis=0)
        entry_id = lax.broadcasted_iota(jnp.int32, scores.shape, 0)
        picked = jnp.sum(jnp.where(entry_id == offset[None, :], scores, 0.0), axis=0)
    answer = jnp.stack([peak, total, picked]).reshape(3, shards, CAP).transpose(1, 0, 2)
    answer = exchange(answer.reshape(shards, 3 * CAP), SEQ).reshape(shards, 3, CAP).transpose(1, 0, 2)
    peak, total, picked = answer.reshape(3, members)
    with jax.named_scope("combine"):
        member = token[:, None] == jnp.arange(tokens, dtype=jnp.int32)[None, :]
        local_peak = jnp.max(jnp.where(member, peak[:, None], floor_value), axis=0)
        scaled = jnp.exp(jnp.where(member, peak[:, None] - local_peak[None, :], floor_value))
        local_total = jnp.sum(scaled * total[:, None], axis=0)
        local_pick = jnp.sum(jnp.where(member, picked[:, None], 0.0), axis=0)
        local = jnp.stack([local_peak, local_total, local_pick])
    every = share(local, TEN)
    top = jnp.max(every[:, 0], axis=0)
    summed = jnp.sum(every[:, 1] * jnp.exp(every[:, 0] - top[None, :]), axis=0)
    chosen = jnp.sum(every[:, 2], axis=0)
    return chosen - top - jnp.log(summed)


def solution(mesh):
    fine = Mesh(mesh.devices.reshape(4, 8, 8, 2), ("x", "z", "y", "core"))
    seq, tensor = ("x", "z"), ("y", "core")
    return jax.shard_map(
        per_device,
        mesh=fine,
        in_specs=(
            P(seq, tensor),
            P(seq, tensor),
            P(),
            P(seq + tensor, None),
            P(seq),
            P(seq),
            P(seq, None),
            P(seq),
        ),
        out_specs=P(seq),
        check_vma=False,
    )
```
